32 devices in a mesh: groups: 2 (over x), tp: 16 (over z, y, core).
Axes of the slice: x: 2, y: 2, z: 4, core: 2. Of those that a mesh axis runs over, the one named last changes fastest.
Arguments:
- queries: bfloat16 [512, 8192], P('groups', 'tp'), parts along dimension 0, may hold values from -200 to 200, as said below
- cache: bfloat16 [16, 16384, 256], P('tp', 'groups'), parts along dimension 1, may hold values from -8 to 8, as said below
- offset: int32 [2], P('groups'), parts along dimension 0, may hold values from 4096 to 7936
- out_weight: bfloat16 [8192, 16384], P('tp'), may hold values from -3 to 3
- residual: bfloat16 [512, 16384], P(('groups', 'tp')), parts along dimension 0, may hold values from -60 to 60
- term_exp: int32 [16, 512, 128], P('tp', 'groups'), parts along dimension 1, may hold values from -13 to -7
- code_exp: int32 [512, 128], P('groups'), parts along dimension 0, may hold values from -9 to -4
- gain: float32 [16384], replicated, may hold values from 0.1 to 1.9
Outputs:
- mixed: bfloat16 [512, 16384], P('groups'), parts along dimension 0
- stream: bfloat16 [512, 16384], P(('groups', 'tp')), parts along dimension 0
The draws below stay inside these ranges and needn't reach their ends.
There are 2 independent parts, one for each index of `groups`. The reference program is written for one: setup_inputs(seed, part) draws one part's arguments, and reference() takes and returns one part's arrays. A program takes and returns all parts, laid end to end along the dimension named above; an argument that names none is the same for every part. Nothing has to cross between parts.
Inputs may be any that keep to these rules, and one draw needn't show every extreme that they name: `queries`: mostly values of about unit size, with possibly a few much larger entries. `cache`: copies for the devices of one key and value head are equal.
All inputs are finite; a program needn't handle non-finite values.
Results may differ from the reference program's by a relative error of at most 0.0095.
Values may be sent and summed in bfloat16 or wider, within the bound.
No kernel may reach another device: no remote copies, remote signals or barrier semaphores. Data moves between devices by JAX's collectives and lax.ppermute only.
A program may use at most 256 MiB of HBM per device.

```python
import math
import jax
import jax.numpy as jnp
from jax import lax

D = 16384
HD = 128
HQ_DEV = 4
KV_HEADS = 8
CTX = 8192
HEADS = 64
TOKENS = 256
BLOCKS = 128
N_TP = 16


def shared_keys(key):
    keys = jax.random.normal(jax.random.fold_in(key, 101), (KV_HEADS, CTX, HD), jnp.float32)
    return keys


def draw_cache(key, part):
    keys = shared_keys(key)
    key = jax.random.fold_in(key, 7)
    values = jax.random.normal(key, (KV_HEADS, CTX, HD), jnp.float32)
    joined = jnp.concatenate([keys, values], axis=2)
    joined = jnp.clip(joined, -8.0, 8.0)
    return jnp.repeat(joined, N_TP // KV_HEADS, axis=0).astype(jnp.bfloat16)


def draw_queries(key, part):
    key = jax.random.fold_in(key, 9)
    values = jax.random.normal(key, (TOKENS, HEADS, HD), jnp.float32)
    values = jnp.clip(values, -200.0, 200.0)
    return values.reshape(TOKENS, HEADS * HD).astype(jnp.bfloat16)


def draw_residual(key, part):
    key = jax.random.fold_in(key, 11)
    first, second, third = jax.random.split(key, 3)
    row_scale = jnp.exp(jax.random.uniform(first, (TOKENS, 1), jnp.float32, math.log(0.32), math.log(3.2)))
    rising = 3.0 ** (jnp.arange(D).astype(jnp.float32) / D)
    col_scale = rising[None, :] * jnp.exp(jax.random.uniform(second, (1, D), jnp.float32, math.log(0.56), math.log(1.8)))
    base = jax.random.normal(third, (TOKENS, D), jnp.float32)
    values = jnp.clip(0.5 * base * row_scale * col_scale, -60.0, 60.0)
    return values.astype(jnp.bfloat16)


def plant(drawn, rng, least, top_value):
    dims = drawn.shape
    place = [jax.random.randint(jax.random.fold_in(rng, axis), (), 0, dims[axis]) for axis in range(len(dims))]
    drawn = drawn.at[tuple(place)].set(least)
    longest = dims.index(max(dims))
    place[longest] = (place[longest] + 1) % dims[longest]
    return drawn.at[tuple(place)].set(top_value)


def level_of(rng, shape, shards, least, high):
    def one(dim, blocks):
        draws = jax.random.uniform(jax.random.fold_in(jax.random.fold_in(rng, 6), dim), (blocks,), jnp.float32, least / len(shards), high / len(shards))
        return jnp.repeat(jnp.exp(draws), shape[dim] // blocks).reshape((-1,) + (1,) * (len(shape) - dim - 1))

    loudness = one(*shards[0])
    for cut in shards[1:]:
        loudness = loudness * one(*cut)
    return loudness


def gaussian(key, dims, scale, limit, cuts=(), dtype=jnp.bfloat16):
    factor_of = level_of(key, dims, cuts, -0.22, 0.18) if cuts else 1.0
    values = jax.random.normal(key, dims, jnp.float32) * scale * factor_of
    return jnp.minimum(jnp.maximum(values, -limit), limit).astype(dtype)


def setup_inputs(seed: int = 0, part: int = 0) -> dict:
    key_list = jax.random.split(jax.random.key(seed), 9)
    part_keys = jax.random.split(jax.random.fold_in(key_list[8], part), 9)
    queries = draw_queries(jax.random.fold_in(jax.random.fold_in(key_list[8], part), 71), part)
    cache = draw_cache(jax.random.fold_in(jax.random.fold_in(key_list[8], part), 71), part)
    offset = jax.random.randint(part_keys[2], (1,), CTX // 2, CTX - TOKENS + 1).astype(jnp.int32)
    out_weight = gaussian(key_list[3], (HEADS * HD, D), (max(1, 4 * HQ_DEV * HD * N_TP // CTX)) ** -0.5, 3.0, ((0, 16),))
    residual = draw_residual(jax.random.fold_in(jax.random.fold_in(key_list[8], part), 71), part)
    term_exp = plant(jax.random.randint(part_keys[5], (N_TP, TOKENS, BLOCKS), -13, -6), jax.random.fold_in(part_keys[5], 1), -13, (-6) - 1).astype(jnp.int32)
    code_exp = plant(jax.random.randint(part_keys[6], (TOKENS, BLOCKS), -9, -3), jax.random.fold_in(part_keys[6], 1), -9, (-3) - 1).astype(jnp.int32)
    gain = jnp.clip(1.0 + 0.18 * jax.random.normal(key_list[7], (D,), jnp.float32), 0.1, 1.9)
    return {"queries": queries, "cache": cache, "offset": offset, "out_weight": out_weight, "residual": residual, "term_exp": term_exp, "code_exp": code_exp, "gain": gain}


def powers(exps):
    magnitude = jnp.abs(exps)
    result = jnp.ones(exps.shape, jnp.float32)
    for bit in range(6):
        chosen = magnitude // 2 ** bit % 2 == 1
        result = result * jnp.where(chosen, jnp.float32(2.0 ** 2 ** bit), jnp.float32(1.0))
    return jnp.where(exps < 0, 1.0 / result, result)

def encode(values, exps):
    rows, cols = values.shape
    blocks = exps.shape[1]
    scale = powers(exps)[:, :, None]
    shaped = values.reshape(rows, blocks, cols // blocks) / scale
    return jnp.clip(shaped, -448.0, 448.0).astype(jnp.bfloat16).reshape(rows, cols)

def decode(codes, exps):
    rows, cols = codes.shape
    blocks = exps.shape[1]
    scale = powers(exps)[:, :, None]
    return (codes.astype(jnp.float32).reshape(rows, blocks, cols // blocks) * scale).reshape(rows, cols)

def restored(values, exps):
    codes = lax.optimization_barrier(encode(values, exps))
    return decode(codes, exps)

def attend(query_rows, key_values, start):
    rows = query_rows.shape[0]
    head = key_values.shape[1] // 2
    heads = query_rows.shape[1] // head
    stacked = query_rows.reshape(rows, heads, head).transpose(1, 0, 2)
    keys = key_values[:, :head]
    values = key_values[:, head:]
    query_pos = start + jnp.arange(rows).astype(jnp.int32)
    key_pos = jnp.arange(keys.shape[0]).astype(jnp.int32)
    seen = key_pos[None, :] <= query_pos[:, None]

    def one_head(single):
        scores = lax.dot_general(single, keys, (((1,), (1,)), ((), ())), preferred_element_type=jnp.float32)
        scores = scores * head ** (-0.5)
        scores = jnp.where(seen, scores, jnp.float32(-1e+30))
        top = lax.optimization_barrier(jnp.max(scores, axis=1, keepdims=True))
        weights = jnp.exp(scores - top)
        probs = (weights / lax.optimization_barrier(jnp.sum(weights, axis=1, keepdims=True))).astype(jnp.bfloat16)
        return jnp.dot(probs, values, preferred_element_type=jnp.float32).astype(jnp.bfloat16)
    mixed = lax.map(one_head, stacked)
    return mixed.transpose(1, 0, 2).reshape(rows, heads * head)

def reference(queries, cache, offset, out_weight, residual, term_exp, code_exp, gain):
    span = HQ_DEV * HD
    start = offset[0]

    def add_term(index, total):
        index = jnp.asarray(index).astype(jnp.int32)
        query_rows = lax.dynamic_slice_in_dim(queries, index * span, span, 1)
        key_values = lax.dynamic_index_in_dim(cache, index, 0, keepdims=False)
        weight_rows = lax.dynamic_slice_in_dim(out_weight, index * span, span, 0)
        exps = lax.dynamic_index_in_dim(term_exp, index, 0, keepdims=False)
        attn = attend(query_rows, key_values, start)
        partial_out = jnp.dot(attn, weight_rows, preferred_element_type=jnp.float32)
        return total + restored(partial_out, exps)
    summed = lax.fori_loop(0, N_TP, add_term, jnp.zeros((TOKENS, D), jnp.float32))
    stream = (summed + residual.astype(jnp.float32)).astype(jnp.bfloat16)
    wide = stream.astype(jnp.float32)
    inverse = lax.rsqrt(lax.optimization_barrier(jnp.mean(wide * wide, axis=1, keepdims=True)) + 1e-05)
    normed = wide * inverse * gain
    codes = lax.optimization_barrier(encode(normed, code_exp))
    mixed = decode(codes, code_exp).astype(jnp.bfloat16)
    return (mixed, stream)
```

```python
import jax
import jax.numpy as jnp
from jax import lax
from jax.sharding import PartitionSpec as P

CHUNKS = 4


def powers(exps):
    magnitude = jnp.abs(exps)
    result = jnp.ones(exps.shape, jnp.float32)
    for bit in range(6):
        chosen = magnitude // 2**bit % 2 == 1
        result = result * jnp.where(chosen, jnp.float32(2.0**2**bit), jnp.float32(1.0))
    return jnp.where(exps < 0, 1.0 / result, result)


def attend(query_rows, key_values, start):
    rows = query_rows.shape[0]
    head = key_values.shape[1] // 2
    heads = query_rows.shape[1] // head
    stacked = query_rows.reshape(rows, heads, head).transpose(1, 0, 2)
    keys = key_values[:, :head]
    values = key_values[:, head:]
    query_pos = start + jnp.arange(rows)
    key_pos = jnp.arange(keys.shape[0])
    seen = key_pos[None, :] <= query_pos[:, None]

    def one_head(single):
        scores = lax.dot_general(
            single, keys, (((1,), (1,)), ((), ())), preferred_element_type=jnp.float32
        )
        scores = scores * head ** (-0.5)
        scores = jnp.where(seen, scores, jnp.float32(-1e30))
        top = jnp.max(scores, axis=1, keepdims=True)
        weights = jnp.exp(scores - top)
        probs = (weights / jnp.sum(weights, axis=1, keepdims=True)).astype(jnp.bfloat16)
        return jnp.dot(probs, values, preferred_element_type=jnp.float32).astype(jnp.bfloat16)

    mixed = lax.map(one_head, stacked)
    return mixed.transpose(1, 0, 2).reshape(rows, heads * head)


def to_relative(x, order, me):
    n = len(order)
    rows = x.shape[0]
    block = rows // 2**n
    shaped = x.reshape((2,) * n + (block,) + x.shape[1:])
    perm = tuple(n - 1 - b for b in order) + tuple(range(n, shaped.ndim))
    shaped = shaped.transpose(perm)
    for axis, b in enumerate(order):
        shaped = jnp.where((me >> b) & 1 == 1, jnp.flip(shaped, axis), shaped)
    return shaped.reshape(x.shape)


def from_relative(x, order, me):
    n = len(order)
    rows = x.shape[0]
    block = rows // 2**n
    shaped = x.reshape((2,) * n + (block,) + x.shape[1:])
    for axis, b in enumerate(order):
        shaped = jnp.where((me >> b) & 1 == 1, jnp.flip(shaped, axis), shaped)
    inverse = [0] * n
    for axis, b in enumerate(order):
        inverse[n - 1 - b] = axis
    shaped = shaped.transpose(tuple(inverse) + tuple(range(n, shaped.ndim)))
    return shaped.reshape(x.shape)


def per_device(queries, cache, offset, out_weight, residual, term_exp, code_exp, gain):
    me = lax.axis_index("tp")
    parts = lax.axis_size("tp")
    bits = parts.bit_length() - 1
    block = residual.shape[0]
    width = residual.shape[1]
    blocks = code_exp.shape[1]
    group = width // blocks
    cols = width // CHUNKS
    bcols = blocks // CHUNKS

    def flip(x, b):
        return lax.ppermute(x, "tp", [(i, i ^ (1 << b)) for i in range(parts)])

    order_a = list(range(bits))
    order_b = [0, 2, 1] + list(range(3, bits))
    orders = [order_b] + [order_a] * (CHUNKS - 1)

    attn = attend(queries, cache[0], offset[0])
    limit = powers(term_exp[0]) * 448.0
    attn_of = {}
    limit_of = {}
    for name, order in (("a", order_a), ("b", order_b)):
        attn_of[name] = to_relative(attn, order, me)
        limit_of[name] = to_relative(limit, order, me)

    sums = []
    for j in range(CHUNKS):
        order = orders[j]
        name = "b" if order is order_b else "a"
        part = jnp.dot(
            attn_of[name], out_weight[:, j * cols : (j + 1) * cols], preferred_element_type=jnp.float32
        )
        rows = part.shape[0]
        lim = limit_of[name][:, j * bcols : (j + 1) * bcols, None]
        part = jnp.clip(part.reshape(rows, bcols, group), -lim, lim).reshape(rows, cols)
        part = part.astype(jnp.bfloat16)
        for step, b in enumerate(order):
            half = part.shape[0] // 2
            came = flip(part[half:], b)
            part = part[:half].astype(jnp.float32) + came.astype(jnp.float32)
            if step < bits - 1:
                part = part.astype(jnp.bfloat16)
        sums.append(part)
    summed = jnp.concatenate(sums, axis=1)
    stream = (summed + residual.astype(jnp.float32)).astype(jnp.bfloat16)
    wide = stream.astype(jnp.float32)
    inverse = lax.rsqrt(jnp.mean(wide * wide, axis=1, keepdims=True) + 1e-05)
    exps = lax.dynamic_slice_in_dim(code_exp, me * block, block, 0)
    cap = (powers(exps) * 448.0)[:, :, None]
    normed = (wide * inverse * gain[None, :]).reshape(block, blocks, group)
    mixed = jnp.clip(normed, -cap, cap).reshape(block, width).astype(jnp.bfloat16)

    outs = []
    for j in range(CHUNKS):
        order = orders[j]
        held = mixed[:, j * cols : (j + 1) * cols]
        for b in reversed(order):
            held = jnp.concatenate([held, flip(held, b)], axis=0)
        outs.append(from_relative(held, order, me))
    return (jnp.concatenate(outs, axis=1), stream)


def solution(mesh):
    in_specs = (
        P("groups", "tp"),
        P("tp", "groups", None),
        P("groups"),
        P("tp", None),
        P(("groups", "tp"), None),
        P("tp", "groups", None),
        P("groups", None),
        P(),
    )
    out_specs = (P("groups", None), P(("groups", "tp"), None))
    return jax.shard_map(
        per_device, mesh=mesh, in_specs=in_specs, out_specs=out_specs, check_vma=False
    )
```

```python
import functools

import jax
import jax.numpy as jnp
from jax import lax
from jax.experimental import pallas as pl
from jax.experimental.pallas import tpu as pltpu
from jax.sharding import PartitionSpec as P

CHUNKS = 4
KEY_BLOCK = 2048
TILE = 1024
CODE_TOP = 448.0
LOG2E = 1.4426950408889634


def powers(exps):
    magnitude = jnp.abs(exps)
    result = jnp.ones(exps.shape, jnp.float32)
    for bit in range(6):
        chosen = (magnitude >> bit) & 1 == 1
        result = result * jnp.where(chosen, jnp.float32(2.0**2**bit), jnp.float32(1.0))
    return jnp.where(exps < 0, 1.0 / result, result)


def attention_kernel(
    start_ref, place_ref, q_ref, kv_ref, exp_ref, *refs, key_block, heads, head, n_orders
):
    attn_refs = refs[:n_orders]
    limit_refs = refs[n_orders : 2 * n_orders]
    top_ref, acc_ref = refs[2 * n_orders :]
    step = pl.program_id(0)
    start = start_ref[0]
    rows = q_ref.shape[0]
    n_blocks = place_ref.shape[1]
    block = rows // n_blocks
    coef = head**-0.5 * LOG2E

    @pl.when(step == 0)
    def _():
        top_ref[...] = jnp.full_like(top_ref, -1e30)
        acc_ref[...] = jnp.zeros_like(acc_ref)
        limit = powers(exp_ref[0]) * CODE_TOP
        for i in range(n_blocks):
            for o in range(n_orders):
                to = pl.ds(pl.multiple_of(place_ref[o, i] * block, block), block)
                limit_refs[o][to, :] = limit[i * block : (i + 1) * block]

    def attend(masked):
        keys = kv_ref[0, :, :head]
        ones = jnp.ones((key_block, head), jnp.bfloat16)
        values = jnp.concatenate([kv_ref[0, :, head:], ones], axis=1)
        if masked:
            row = lax.broadcasted_iota(jnp.int32, (rows, key_block), 0)
            col = lax.broadcasted_iota(jnp.int32, (rows, key_block), 1)
            seen = col - row <= start - step * key_block
        for h in range(heads):
            scores = lax.dot_general(
                q_ref[:, h * head : (h + 1) * head],
                keys,
                (((1,), (1,)), ((), ())),
                preferred_element_type=jnp.float32,
            )
            if masked:
                scores = jnp.where(seen, scores, jnp.float32(-1e30))
            before = top_ref[h]
            top = jnp.maximum(before, jnp.max(scores, axis=1, keepdims=True))
            weights = jnp.exp2((scores - top[:, :1]) * coef).astype(jnp.bfloat16)
            fade = jnp.exp2((before - top) * coef)
            got = jnp.dot(weights, values, preferred_element_type=jnp.float32)
            acc_ref[h] = acc_ref[h] * jnp.concatenate([fade, fade], axis=1) + got
            top_ref[h] = top

    first = step * key_block
    past = first + key_block - 1 > start

    @pl.when(jnp.logical_and(past, first <= start + rows - 1))
    def _():
        attend(True)

    @pl.when(jnp.logical_not(past))
    def _():
        attend(False)

    @pl.when(step == pl.num_programs(0) - 1)
    def _():
        for h in range(heads):
            acc = acc_ref[h]
            out = (acc[:, :head] / acc[:, head:]).astype(jnp.bfloat16)
            for i in range(n_blocks):
                for o in range(n_orders):
                    to = pl.ds(pl.multiple_of(place_ref[o, i] * block, block), block)
                    attn_refs[o][to, h * head : (h + 1) * head] = out[i * block : (i + 1) * block]


def attention(start, places, queries, cache, term_exp):
    rows, span = queries.shape
    context, head = cache.shape[1], cache.shape[2] // 2
    heads = span // head
    n_orders = places.shape[0]
    blocks = term_exp.shape[2]
    key_block = min(KEY_BLOCK, context)

    def cache_block(step, start_ref, place_ref):
        return (0, jnp.minimum(step, (start_ref[0] + rows - 1) // key_block), 0)

    def whole(*shape):
        return pl.BlockSpec(shape, lambda step, start_ref, place_ref: (0,) * len(shape))

    return pl.pallas_call(
        functools.partial(
            attention_kernel, key_block=key_block, heads=heads, head=head, n_orders=n_orders
        ),
        grid_spec=pltpu.PrefetchScalarGridSpec(
            num_scalar_prefetch=2,
            grid=(context // key_block,),
            in_specs=[
                whole(rows, span),
                pl.BlockSpec((1, key_block, 2 * head), cache_block),
                whole(1, rows, blocks),
            ],
            out_specs=[whole(rows, span)] * n_orders + [whole(rows, blocks)] * n_orders,
            scratch_shapes=[
                pltpu.VMEM((heads, rows, head), jnp.float32),
                pltpu.VMEM((heads, rows, 2 * head), jnp.float32),
            ],
        ),
        out_shape=[jax.ShapeDtypeStruct((rows, span), jnp.bfloat16)] * n_orders
        + [jax.ShapeDtypeStruct((rows, blocks), jnp.float32)] * n_orders,
        compiler_params=pltpu.CompilerParams(vmem_limit_bytes=48 << 20),
        name="attention",
    )(start, places, queries, cache, term_exp)


def project_kernel(attn_ref, weight_ref, limit_ref, keep_ref, send_ref, *, first, group):
    step = pl.program_id(0)
    half = keep_ref.shape[0]
    lanes = limit_ref.shape[1]
    per = weight_ref.shape[1] // group
    shift = lax.rem(lanes - (first + step * per), lanes)
    limit = pltpu.roll(limit_ref[...], shift, 1)
    got = jnp.dot(attn_ref[...], weight_ref[...], preferred_element_type=jnp.float32)
    for b in range(per):
        cut = slice(b * group, (b + 1) * group)
        bound = jnp.broadcast_to(limit[:, b : b + 1], (2 * half, group))
        part = jnp.minimum(jnp.maximum(got[:, cut], -bound), bound).astype(jnp.bfloat16)
        keep_ref[:, cut] = part[:half]
        send_ref[:, cut] = part[half:]


def project(attn, out_weight, limit, first_col, cols):
    rows, span = attn.shape
    group = out_weight.shape[1] // limit.shape[1]
    half = rows // 2
    base = first_col // TILE
    return pl.pallas_call(
        functools.partial(project_kernel, first=first_col // group, group=group),
        grid=(cols // TILE,),
        in_specs=[
            pl.BlockSpec((rows, span), lambda i: (0, 0)),
            pl.BlockSpec((span, TILE), lambda i: (0, base + i)),
            pl.BlockSpec(limit.shape, lambda i: (0, 0)),
        ],
        out_specs=[pl.BlockSpec((half, TILE), lambda i: (0, i))] * 2,
        out_shape=[jax.ShapeDtypeStruct((half, cols), jnp.bfloat16)] * 2,
        compiler_params=pltpu.CompilerParams(vmem_limit_bytes=32 << 20),
        cost_estimate=pl.CostEstimate(
            flops=2 * rows * span * cols,
            bytes_accessed=2 * (span * cols + rows * span + rows * cols),
            transcendentals=0,
        ),
        name="project",
    )(attn, out_weight, limit)


def from_relative(x, order, me):
    n = len(order)
    rows = x.shape[0]
    block = rows // 2**n
    shaped = x.reshape((2,) * n + (block,) + x.shape[1:])
    for axis, b in enumerate(order):
        shaped = jnp.where((me >> b) & 1 == 1, jnp.flip(shaped, axis), shaped)
    inverse = [0] * n
    for axis, b in enumerate(order):
        inverse[n - 1 - b] = axis
    shaped = shaped.transpose(tuple(inverse) + tuple(range(n, shaped.ndim)))
    return shaped.reshape(x.shape)


def per_device(queries, cache, offset, out_weight, residual, term_exp, code_exp, gain):
    me = lax.axis_index("tp")
    parts = lax.axis_size("tp")
    bits = parts.bit_length() - 1
    block, width = residual.shape
    blocks = code_exp.shape[1]
    group = width // blocks
    cols = width // CHUNKS

    def flip(x, b):
        return lax.ppermute(x, "tp", [(i, i ^ (1 << b)) for i in range(parts)])

    order_a = list(range(bits))
    order_b = [0, 2, 1] + list(range(3, bits))
    kinds = [order_a, order_b]
    uses = [1] + [0] * (CHUNKS - 1)

    apart = jnp.arange(parts, dtype=jnp.int32) ^ me
    places = jnp.stack(
        [sum(((apart >> b) & 1) << (bits - 1 - k) for k, b in enumerate(order)) for order in kinds]
    )
    got = attention(offset, places, queries, cache, term_exp)
    attns, limits = got[: len(kinds)], got[len(kinds) :]

    sums = []
    for j in range(CHUNKS):
        kind = uses[j]
        keep, send = project(attns[kind], out_weight, limits[kind], j * cols, cols)
        for step, b in enumerate(kinds[kind]):
            came = flip(send, b)
            if step < bits - 1:
                half = keep.shape[0] // 2
                send = (keep[half:].astype(jnp.float32) + came[half:].astype(jnp.float32)).astype(jnp.bfloat16)
                keep = (keep[:half].astype(jnp.float32) + came[:half].astype(jnp.float32)).astype(jnp.bfloat16)
            else:
                keep = keep.astype(jnp.float32) + came.astype(jnp.float32)
        sums.append(keep)
    summed = jnp.concatenate(sums, axis=1)
    stream = (summed + residual.astype(jnp.float32)).astype(jnp.bfloat16)
    wide = stream.astype(jnp.float32)
    inverse = lax.rsqrt(jnp.mean(wide * wide, axis=1, keepdims=True) + 1e-05)
    exps = lax.dynamic_slice_in_dim(code_exp, me * block, block, 0)
    cap = (powers(exps) * CODE_TOP)[:, :, None]
    normed = (wide * inverse * gain[None, :]).reshape(block, blocks, group)
    mixed = jnp.clip(normed, -cap, cap).reshape(block, width).astype(jnp.bfloat16)

    outs = []
    for j in range(CHUNKS):
        order = kinds[uses[j]]
        held = mixed[:, j * cols : (j + 1) * cols]
        for b in reversed(order):
            held = jnp.concatenate([held, flip(held, b)], axis=0)
        outs.append(from_relative(held, order, me))
    return (jnp.concatenate(outs, axis=1), stream)


def solution(mesh):
    in_specs = (
        P("groups", "tp"),
        P("tp", "groups", None),
        P("groups"),
        P("tp", None),
        P(("groups", "tp"), None),
        P("tp", "groups", None),
        P("groups", None),
        P(),
    )
    out_specs = (P("groups", None), P(("groups", "tp"), None))
    return jax.shard_map(
        per_device, mesh=mesh, in_specs=in_specs, out_specs=out_specs, check_vma=False
    )
```

```python
import functools

import jax
import jax.numpy as jnp
from jax import lax
from jax.experimental import pallas as pl
from jax.experimental.pallas import tpu as pltpu
from jax.sharding import PartitionSpec as P

CHUNKS = 4
KEY_BLOCK = 2048
TILE = 1024
PUT_COST = 4
CODE_TOP = 448.0
LOG2E = 1.4426950408889634


def powers(exps):
    magnitude = jnp.abs(exps)
    result = jnp.ones(exps.shape, jnp.float32)
    for bit in range(6):
        chosen = (magnitude >> bit) & 1 == 1
        result = result * jnp.where(chosen, jnp.float32(2.0**2**bit), jnp.float32(1.0))
    return jnp.where(exps < 0, 1.0 / result, result)


def partial_kernel(
    start_ref, q_ref, kv_ref, exp_ref, weight_ref, *refs, key_block, heads, head, kinds, orders
):
    n_chunks = len(kinds)
    outs = [(refs[2 * j], refs[2 * j + 1]) for j in range(n_chunks)]
    top_ref, acc_ref, limit_ref, attn_ref, held_ref, stage_ref, in_sems, out_sems = refs[2 * n_chunks :]
    step = pl.program_id(0)
    start = start_ref[0]
    rows = q_ref.shape[0]
    n_orders, n_blocks = len(orders), 2 ** len(orders[0])
    me = lax.axis_index("tp")
    block = rows // n_blocks
    coef = head**-0.5 * LOG2E
    n_tiles, _, tile = held_ref.shape
    lanes = limit_ref.shape[2]
    group = weight_ref.shape[1] // lanes
    per = tile // group
    half = rows // 2

    def weight_copy(t):
        return pltpu.make_async_copy(
            weight_ref.at[:, pl.ds(pl.multiple_of(t * tile, tile), tile)], held_ref.at[t], in_sems.at[t]
        )

    @pl.when(step == 0)
    def _():
        for t in range(n_tiles):
            weight_copy(t).start()
        top_ref[...] = jnp.full_like(top_ref, -1e30)
        acc_ref[...] = jnp.zeros_like(acc_ref)
        limit = powers(exp_ref[0]) * CODE_TOP
        for i in range(n_blocks):
            for o in range(n_orders):
                to = pl.ds(pl.multiple_of(place_of(i ^ me, orders[o]) * block, block), block)
                limit_ref[o, to, :] = limit[i * block : (i + 1) * block]

    def attend(masked):
        keys = kv_ref[0, :, :head]
        ones = jnp.ones((key_block, head), jnp.bfloat16)
        values = jnp.concatenate([kv_ref[0, :, head:], ones], axis=1)
        if masked:
            row = lax.broadcasted_iota(jnp.int32, (rows, key_block), 0)
            col = lax.broadcasted_iota(jnp.int32, (rows, key_block), 1)
            seen = col - row <= start - step * key_block
        for h in range(heads):
            scores = lax.dot_general(
                q_ref[:, h * head : (h + 1) * head],
                keys,
                (((1,), (1,)), ((), ())),
                preferred_element_type=jnp.float32,
            )
            if masked:
                scores = jnp.where(seen, scores, jnp.float32(-1e30))
            before = top_ref[h]
            top = jnp.maximum(before, jnp.max(scores, axis=1, keepdims=True))
            weights = jnp.exp2((scores - top[:, :1]) * coef).astype(jnp.bfloat16)
            fade = jnp.exp2((before - top) * coef)
            got = jnp.dot(weights, values, preferred_element_type=jnp.float32)
            acc_ref[h] = acc_ref[h] * jnp.concatenate([fade, fade], axis=1) + got
            top_ref[h] = top

    first = step * key_block
    past = first + key_block - 1 > start

    @pl.when(jnp.logical_and(past, first <= start + rows - 1))
    def _():
        attend(True)

    @pl.when(jnp.logical_not(past))
    def _():
        attend(False)

    @pl.when(step == pl.num_programs(0) - 1)
    def _():
        for h in range(heads):
            acc = acc_ref[h]
            out = (acc[:, :head] / acc[:, head:]).astype(jnp.bfloat16)
            for i in range(n_blocks):
                for o in range(n_orders):
                    to = pl.ds(pl.multiple_of(place_of(i ^ me, orders[o]) * block, block), block)
                    attn_ref[o, to, h * head : (h + 1) * head] = out[i * block : (i + 1) * block]

        per_chunk = n_tiles // n_chunks
        slots = stage_ref.shape[0]
        waiting = {}
        for t in range(n_tiles):
            j, within = t // per_chunk, t % per_chunk
            slot = t % slots
            weight_copy(t).wait()
            for copy in waiting.pop(slot, ()):
                copy.wait()
            limit = limit_ref[kinds[j]]
            got = jnp.dot(attn_ref[kinds[j]], held_ref[t], preferred_element_type=jnp.float32)
            for b in range(per):
                cut = slice(b * group, (b + 1) * group)
                bound = jnp.broadcast_to(limit[:, t * per + b : t * per + b + 1], (rows, group))
                part = jnp.minimum(jnp.maximum(got[:, cut], -bound), bound)
                stage_ref[slot, :, cut] = part.astype(jnp.bfloat16)
            copies = []
            for side in range(2):
                copies.append(
                    pltpu.make_async_copy(
                        stage_ref.at[slot, pl.ds(side * half, half), :],
                        outs[j][side].at[:, pl.ds(within * tile, tile)],
                        out_sems.at[slot, side],
                    )
                )
                copies[-1].start()
            waiting[slot] = copies
        for copies in waiting.values():
            for copy in copies:
                copy.wait()


def partials(start, queries, cache, term_exp, out_weight, kinds, orders):
    rows, span = queries.shape
    context, head = cache.shape[1], cache.shape[2] // 2
    heads = span // head
    n_orders = len(orders)
    blocks = term_exp.shape[2]
    width = out_weight.shape[1]
    n_tiles = width // TILE
    key_block = min(KEY_BLOCK, context)
    half, cols = rows // 2, width // len(kinds)

    def cache_block(step, start_ref):
        return (0, jnp.minimum(step, (start_ref[0] + rows - 1) // key_block), 0)

    def whole(*shape):
        return pl.BlockSpec(shape, lambda step, start_ref: (0,) * len(shape))

    anywhere = pl.BlockSpec(memory_space=pl.ANY)
    got = pl.pallas_call(
        functools.partial(partial_kernel, key_block=key_block, heads=heads, head=head, kinds=kinds, orders=orders),
        grid_spec=pltpu.PrefetchScalarGridSpec(
            num_scalar_prefetch=1,
            grid=(context // key_block,),
            in_specs=[
                whole(rows, span),
                pl.BlockSpec((1, key_block, 2 * head), cache_block),
                whole(1, rows, blocks),
                anywhere,
            ],
            out_specs=[anywhere] * (2 * len(kinds)),
            scratch_shapes=[
                pltpu.VMEM((heads, rows, head), jnp.float32),
                pltpu.VMEM((heads, rows, 2 * head), jnp.float32),
                pltpu.VMEM((n_orders, rows, blocks), jnp.float32),
                pltpu.VMEM((n_orders, rows, span), jnp.bfloat16),
                pltpu.VMEM((n_tiles, span, TILE), jnp.bfloat16),
                pltpu.VMEM((4, rows, TILE), jnp.bfloat16),
                pltpu.SemaphoreType.DMA((n_tiles,)),
                pltpu.SemaphoreType.DMA((4, 2)),
            ],
        ),
        out_shape=[jax.ShapeDtypeStruct((half, cols), jnp.bfloat16)] * (2 * len(kinds)),
        compiler_params=pltpu.CompilerParams(vmem_limit_bytes=58 << 20),
        name="partials",
    )(start, queries, cache, term_exp, out_weight)
    return [(got[2 * j], got[2 * j + 1]) for j in range(len(kinds))]


def place_of(index, order):
    top = len(order) - 1
    return sum(((index >> b) & 1) << (top - k) for k, b in enumerate(order))


def device_of(place, order):
    top = len(order) - 1
    return sum(((place >> (top - k)) & 1) << b for k, b in enumerate(order))


def put_kernel(source_ref, *refs, first, order, base):
    out_ref, stage_ref, in_sems, out_sems = refs[-4:]
    me = lax.axis_index("tp")
    half, cols = source_ref.shape
    block = 2 * half >> len(order)
    reads, writes = [], []
    for i in range(half // block):
        here = pl.ds(i * block, block)
        to = pl.multiple_of((me ^ device_of(base + i, order)) * block, block)
        reads.append(pltpu.make_async_copy(source_ref.at[here, :], stage_ref.at[here, :], in_sems.at[i]))
        writes.append(
            pltpu.make_async_copy(
                stage_ref.at[here, :], out_ref.at[pl.ds(to, block), pl.ds(first, cols)], out_sems.at[i]
            )
        )
    for read in reads:
        read.start()
    for read, write in zip(reads, writes):
        read.wait()
        write.start()
    for write in writes:
        write.wait()


def put(source, out, first, width, order, base):
    half, cols = source.shape
    n = 2 ** len(order) // 2
    anywhere = pl.BlockSpec(memory_space=pl.ANY)
    given = (source,) + (() if out is None else (out,))
    return pl.pallas_call(
        functools.partial(put_kernel, first=first, order=order, base=base),
        in_specs=[anywhere] * len(given),
        out_specs=anywhere,
        scratch_shapes=[
            pltpu.VMEM((half, cols), source.dtype),
            pltpu.SemaphoreType.DMA((n,)),
            pltpu.SemaphoreType.DMA((n,)),
        ],
        out_shape=jax.ShapeDtypeStruct((2 * half, width), source.dtype),
        input_output_aliases={} if out is None else {1: 0},
        cost_estimate=pl.CostEstimate(flops=0, bytes_accessed=PUT_COST * half * cols, transcendentals=0),
        name="put",
    )(*given)


def scatter_plan(bits):
    last = bits - 1
    far = list(range(2, last))
    plan = [(0, 0), (1, 0), (2, 0), (3, 0), (0, 1), (1, 1)] + [(0, s) for s in far]
    plan += [(2, 1)] + [(1, s) for s in far] + [(3, 1)]
    plan += [(1, last)] + [(2, s) for s in far] + [(0, last), (2, last)] + [(3, s) for s in far] + [(3, last)]
    return plan


def gather_plan(bits):
    last = bits - 1
    far = list(range(last - 1, 1, -1))
    plan = [(1, last), (0, last)] + [(1, s) for s in far]
    plan += [(2, last)] + [(2, s) for s in far] + [(3, last), (1, 1)] + [(3, s) for s in far]
    plan += [(1, 0)] + [(0, s) for s in far] + [(2, 1), (2, 0), (0, 1), (0, 0), (3, 1), (3, 0)]
    return plan


def per_device(queries, cache, offset, out_weight, residual, term_exp, code_exp, gain):
    me = lax.axis_index("tp")
    parts = lax.axis_size("tp")
    bits = parts.bit_length() - 1
    block, width = residual.shape
    blocks = code_exp.shape[1]
    group = width // blocks
    cols = width // CHUNKS

    def flip(x, b):
        return lax.ppermute(x, "tp", [(i, i ^ (1 << b)) for i in range(parts)])

    order_a = list(range(bits))
    order_b = [0] + list(range(2, bits)) + [1]
    kinds = [order_a, order_b]
    uses = [1] + [0] * (CHUNKS - 1)

    state = partials(offset, queries, cache, term_exp, out_weight, uses, kinds)

    def held_back(x, others):
        return lax.optimization_barrier((x,) + tuple(others))[0] if others else x

    def merge(keep, came, last=False):
        if last:
            return keep.astype(jnp.float32) + came.astype(jnp.float32), None
        half = keep.shape[0] // 2
        send = (keep[half:].astype(jnp.float32) + came[half:].astype(jnp.float32)).astype(jnp.bfloat16)
        keep = (keep[:half].astype(jnp.float32) + came[:half].astype(jnp.float32)).astype(jnp.bfloat16)
        return keep, send

    last = bits - 1
    dones = []
    for j, step in scatter_plan(bits):
        keep, send = state[j]
        with jax.named_scope(f"rs{j}{step}"):
            came = held_back(flip(send, kinds[uses[j]][step]), dones[-1:])
            state[j] = merge(keep, came, step == last)
            dones.append(state[j][0 if step == last else 1])
    sums = [state[j][0] for j in range(CHUNKS)]
    summed = jnp.concatenate(sums, axis=1)
    stream = (summed + residual.astype(jnp.float32)).astype(jnp.bfloat16)
    wide = stream.astype(jnp.float32)
    inverse = lax.rsqrt(jnp.mean(wide * wide, axis=1, keepdims=True) + 1e-05)
    exps = lax.dynamic_slice_in_dim(code_exp, me * block, block, 0)
    cap = (powers(exps) * CODE_TOP)[:, :, None]
    normed = (wide * inverse * gain[None, :]).reshape(block, blocks, group)
    mixed = jnp.clip(normed, -cap, cap).reshape(block, width).astype(jnp.bfloat16)

    held = {j: mixed[:, j * cols : (j + 1) * cols] for j in range(CHUNKS)}
    out = None
    dones = []
    for j, step in gather_plan(bits):
        kind = uses[j]
        with jax.named_scope(f"ag{j}{step}"):
            came = flip(held[j], kinds[kind][step])
            if step:
                came = held_back(came, dones[-1:])
                held[j] = jnp.concatenate([held[j], came], axis=0)
                dones.append(held[j])
            else:
                for base, source in ((0, held[j]), (parts // 2, came)):
                    out = put(source, out, j * cols, width, kinds[kind], base)
    return (out, stream)


def solution(mesh):
    in_specs = (
        P("groups", "tp"),
        P("tp", "groups", None),
        P("groups"),
        P("tp", None),
        P(("groups", "tp"), None),
        P("tp", "groups", None),
        P("groups", None),
        P(),
    )
    out_specs = (P("groups", None), P(("groups", "tp"), None))
    return jax.shard_map(
        per_device, mesh=mesh, in_specs=in_specs, out_specs=out_specs, check_vma=False
    )
```

```python
import functools

import jax
import jax.numpy as jnp
from jax import lax
from jax.experimental import pallas as pl
from jax.experimental.pallas import tpu as pltpu
from jax.sharding import PartitionSpec as P

WIDTHS = (4, 5, 4, 3)
CHUNKS = len(WIDTHS)
GATHER = (3, 2, 1)
KEY_BLOCK = 2048
TILE = 1024
CODE_TOP = 448.0
LOG2E = 1.4426950408889634


def powers(exps):
    magnitude = jnp.abs(exps)
    result = jnp.ones(exps.shape, jnp.float32)
    for bit in range(6):
        chosen = (magnitude >> bit) & 1 == 1
        result = result * jnp.where(chosen, jnp.float32(2.0**2**bit), jnp.float32(1.0))
    return jnp.where(exps < 0, 1.0 / result, result)


def partial_kernel(
    start_ref, q_ref, kv_ref, exp_ref, weight_ref, *refs, key_block, heads, head, kinds, orders, edges
):
    n_chunks = len(kinds)
    outs = [(refs[2 * j], refs[2 * j + 1]) for j in range(n_chunks)]
    top_ref, acc_ref, limit_ref, attn_ref, held_ref, stage_ref, in_sems, out_sems = refs[2 * n_chunks :]
    step = pl.program_id(0)
    start = start_ref[0]
    rows = q_ref.shape[0]
    n_orders, n_blocks = len(orders), 2 ** len(orders[0])
    me = lax.axis_index("tp")
    block = rows // n_blocks
    coef = head**-0.5 * LOG2E
    n_tiles, _, tile = held_ref.shape
    lanes = limit_ref.shape[2]
    group = weight_ref.shape[1] // lanes
    per = tile // group
    half = rows // 2

    def weight_copy(t):
        return pltpu.make_async_copy(
            weight_ref.at[:, pl.ds(pl.multiple_of(t * tile, tile), tile)], held_ref.at[t], in_sems.at[t]
        )

    @pl.when(step == 0)
    def _():
        for t in range(n_tiles):
            weight_copy(t).start()
        top_ref[...] = jnp.full_like(top_ref, -1e30)
        acc_ref[...] = jnp.zeros_like(acc_ref)
        limit = powers(exp_ref[0]) * CODE_TOP
        for i in range(n_blocks):
            for o in range(n_orders):
                to = pl.ds(pl.multiple_of(place_of(i ^ me, orders[o]) * block, block), block)
                limit_ref[o, to, :] = limit[i * block : (i + 1) * block]

    def attend(masked):
        keys = kv_ref[0, :, :head]
        ones = jnp.ones((key_block, head), jnp.bfloat16)
        values = jnp.concatenate([kv_ref[0, :, head:], ones], axis=1)
        if masked:
            row = lax.broadcasted_iota(jnp.int32, (rows, key_block), 0)
            col = lax.broadcasted_iota(jnp.int32, (rows, key_block), 1)
            seen = col - row <= start - step * key_block
        for h in range(heads):
            scores = lax.dot_general(
                q_ref[:, h * head : (h + 1) * head],
                keys,
                (((1,), (1,)), ((), ())),
                preferred_element_type=jnp.float32,
            )
            if masked:
                scores = jnp.where(seen, scores, jnp.float32(-1e30))
            before = top_ref[h]
            top = jnp.maximum(before, jnp.max(scores, axis=1, keepdims=True))
            weights = jnp.exp2((scores - top[:, :1]) * coef).astype(jnp.bfloat16)
            fade = jnp.exp2((before - top) * coef)
            got = jnp.dot(weights, values, preferred_element_type=jnp.float32)
            acc_ref[h] = acc_ref[h] * jnp.concatenate([fade, fade], axis=1) + got
            top_ref[h] = top

    first = step * key_block
    past = first + key_block - 1 > start

    @pl.when(jnp.logical_and(past, first <= start + rows - 1))
    def _():
        attend(True)

    @pl.when(jnp.logical_not(past))
    def _():
        attend(False)

    @pl.when(step == pl.num_programs(0) - 1)
    def _():
        for h in range(heads):
            acc = acc_ref[h]
            out = (acc[:, :head] / acc[:, head:]).astype(jnp.bfloat16)
            for i in range(n_blocks):
                for o in range(n_orders):
                    to = pl.ds(pl.multiple_of(place_of(i ^ me, orders[o]) * block, block), block)
                    attn_ref[o, to, h * head : (h + 1) * head] = out[i * block : (i + 1) * block]

        writes = []
        for j in range(n_chunks):
            tiles = range(edges[j] // tile, edges[j + 1] // tile)
            for t in tiles:
                weight_copy(t).wait()
            limit = limit_ref[kinds[j]]
            rel = attn_ref[kinds[j]]
            for t in tiles:
                got = jnp.dot(rel, held_ref[t], preferred_element_type=jnp.float32)
                for b in range(per):
                    cut = slice(b * group, (b + 1) * group)
                    to = slice(t * tile + b * group, t * tile + (b + 1) * group)
                    bound = jnp.broadcast_to(limit[:, t * per + b : t * per + b + 1], (rows, group))
                    part = jnp.minimum(jnp.maximum(got[:, cut], -bound), bound)
                    stage_ref[:, to] = part.astype(jnp.bfloat16)
            for side in range(2):
                write = pltpu.make_async_copy(
                    stage_ref.at[pl.ds(side * half, half), pl.ds(edges[j], edges[j + 1] - edges[j])],
                    outs[j][side],
                    out_sems.at[j, side],
                )
                write.start()
                writes.append(write)
        for write in writes:
            write.wait()


def partials(start, queries, cache, term_exp, out_weight, kinds, orders, edges):
    rows, span = queries.shape
    context, head = cache.shape[1], cache.shape[2] // 2
    heads = span // head
    n_orders = len(orders)
    blocks = term_exp.shape[2]
    width = out_weight.shape[1]
    n_tiles = width // TILE
    key_block = min(KEY_BLOCK, context)
    half = rows // 2

    def cache_block(step, start_ref):
        return (0, jnp.minimum(step, (start_ref[0] + rows - 1) // key_block), 0)

    def whole(*shape):
        return pl.BlockSpec(shape, lambda step, start_ref: (0,) * len(shape))

    anywhere = pl.BlockSpec(memory_space=pl.ANY)
    got = pl.pallas_call(
        functools.partial(partial_kernel, key_block=key_block, heads=heads, head=head, kinds=kinds, orders=orders, edges=edges
        ),
        grid_spec=pltpu.PrefetchScalarGridSpec(
            num_scalar_prefetch=1,
            grid=(context // key_block,),
            in_specs=[
                whole(rows, span),
                pl.BlockSpec((1, key_block, 2 * head), cache_block),
                whole(1, rows, blocks),
                anywhere,
            ],
            out_specs=[anywhere] * (2 * len(kinds)),
            scratch_shapes=[
                pltpu.VMEM((heads, rows, head), jnp.float32),
                pltpu.VMEM((heads, rows, 2 * head), jnp.float32),
                pltpu.VMEM((n_orders, rows, blocks), jnp.float32),
                pltpu.VMEM((n_orders, rows, span), jnp.bfloat16),
                pltpu.VMEM((n_tiles, span, TILE), jnp.bfloat16),
                pltpu.VMEM((rows, width), jnp.bfloat16),
                pltpu.SemaphoreType.DMA((n_tiles,)),
                pltpu.SemaphoreType.DMA((len(kinds), 2)),
            ],
        ),
        out_shape=[
            jax.ShapeDtypeStruct((half, edges[i // 2 + 1] - edges[i // 2]), jnp.bfloat16)
            for i in range(2 * len(kinds))
        ],
        compiler_params=pltpu.CompilerParams(vmem_limit_bytes=58 << 20),
        name="partials",
    )(start, queries, cache, term_exp, out_weight)
    return [(got[2 * j], got[2 * j + 1]) for j in range(len(kinds))]


def place_of(index, order):
    top = len(order) - 1
    return sum(((index >> b) & 1) << (top - k) for k, b in enumerate(order))


def put_kernel(*refs, places):
    n = len(places)
    out_ref, stages = refs[-3 - n], refs[-2 - n : -2]
    in_sems, out_sems = refs[-2:]
    me = lax.axis_index("tp")
    reads, writes = [], []
    for i, (at, side, y, core, first) in enumerate(places):
        source = refs[at] if side is None else refs[at].at[side]
        cols = source.shape[-1]
        y = side if y is None else ((me >> 1) & 1) ^ y
        there = out_ref.at[:, y, (me & 1) ^ core, :, pl.ds(first, cols)]
        reads.append(pltpu.make_async_copy(source, stages[i], in_sems.at[i]))
        writes.append(pltpu.make_async_copy(stages[i], there, out_sems.at[i]))
    for read in reads:
        read.start()
    for read, write in zip(reads, writes):
        read.wait()
        write.start()
    for write in writes:
        write.wait()


def put(pieces, out, far, block, width):
    sources, places = [], []
    for array, y, core, first in pieces:
        for side in (None,) if y is not None else range(2):
            places.append((len(sources), side, y, core, first))
        sources.append(array)
    n = len(places)
    sizes = [sources[place[0]].shape[-1] for place in places]
    anywhere = pl.BlockSpec(memory_space=pl.ANY)
    given = sources + ([] if out is None else [out])
    return pl.pallas_call(
        functools.partial(put_kernel, places=places),
        in_specs=[anywhere] * len(given),
        out_specs=anywhere,
        scratch_shapes=[pltpu.VMEM((far, block, cols), sources[0].dtype) for cols in sizes]
        + [
            pltpu.SemaphoreType.DMA((n,)),
            pltpu.SemaphoreType.DMA((n,)),
        ],
        out_shape=jax.ShapeDtypeStruct((far, 2, 2, block, width), sources[0].dtype),
        input_output_aliases={} if out is None else {len(sources): 0},
        compiler_params=pltpu.CompilerParams(vmem_limit_bytes=40 << 20),
        cost_estimate=pl.CostEstimate(
            flops=0, bytes_accessed=4 * far * block * sum(sizes), transcendentals=0
        ),
        name="put",
    )(*given)


def scatter_plan(bits):
    last = bits - 1
    far = list(range(2, last))
    plan = [(0, 0), (1, 0), (2, 0), (3, 0), (0, 1), (1, 1)] + [(0, s) for s in far]
    plan += [(2, 1)] + [(1, s) for s in far] + [(3, 1)]
    plan += [(1, last)] + [(2, s) for s in far] + [(0, last), (2, last)] + [(3, s) for s in far] + [(3, last)]
    return plan


def gather_plan(bits):
    last = bits - 1
    far = list(range(last - 1, 1, -1))
    one, two, three = GATHER
    plan = [(one, last), (0, last)] + [(one, s) for s in far]
    plan += [(two, last)] + [(two, s) for s in far] + [(one, 1), (three, last)] + [(three, s) for s in far]
    plan += [(0, s) for s in far] + [(two, 1), (0, 1), (three, 1)]
    return plan


def per_device(queries, cache, offset, out_weight, residual, term_exp, code_exp, gain):
    me = lax.axis_index("tp")
    parts = lax.axis_size("tp")
    bits = parts.bit_length() - 1
    block, width = residual.shape
    blocks = code_exp.shape[1]
    group = width // blocks
    unit = width // sum(WIDTHS)
    edges = [unit * sum(WIDTHS[:j]) for j in range(CHUNKS + 1)]

    def flip(x, b):
        return lax.ppermute(x, "tp", [(i, i ^ (1 << b)) for i in range(parts)])

    order_a = list(range(bits))
    order_b = [0] + list(range(2, bits)) + [1]
    kinds = [order_a, order_b]
    uses = [1] + [0] * (CHUNKS - 1)

    state = partials(offset, queries, cache, term_exp, out_weight, uses, kinds, edges)

    def held_back(x, others):
        return lax.optimization_barrier((x,) + tuple(others))[0] if others else x

    def merge(keep, came, last=False):
        if last:
            return keep.astype(jnp.float32) + came.astype(jnp.float32), None
        half = keep.shape[0] // 2
        send = (keep[half:].astype(jnp.float32) + came[half:].astype(jnp.float32)).astype(jnp.bfloat16)
        keep = (keep[:half].astype(jnp.float32) + came[:half].astype(jnp.float32)).astype(jnp.bfloat16)
        return keep, send

    last = bits - 1
    dones = []
    for j, step in scatter_plan(bits):
        keep, send = state[j]
        with jax.named_scope(f"rs{j}{step}"):
            came = held_back(flip(send, kinds[uses[j]][step]), dones[-1:])
            state[j] = merge(keep, came, step == last)
            dones.append(state[j][0 if step == last else 1])
    sums = [state[j][0] for j in range(CHUNKS)]
    summed = jnp.concatenate(sums, axis=1)
    stream = (summed + residual.astype(jnp.float32)).astype(jnp.bfloat16)
    wide = stream.astype(jnp.float32)
    inverse = lax.rsqrt(jnp.mean(wide * wide, axis=1, keepdims=True) + 1e-05)
    exps = lax.dynamic_slice_in_dim(code_exp, me * block, block, 0)
    cap = (powers(exps) * CODE_TOP)[:, :, None]
    normed = (wide * inverse * gain[None, :]).reshape(block, blocks, group)
    mixed = jnp.clip(normed, -cap, cap).reshape(block, width).astype(jnp.bfloat16)

    ones = (1,) * (bits - 1)
    held = {j: mixed[:, edges[j] : edges[j + 1]].reshape(ones + (block, -1)) for j in range(CHUNKS)}
    far = parts // 4

    def join(x, came, b):
        upper = (me >> b) & 1 == 1
        axis = 0 if b == 1 else bits - b
        return jnp.concatenate([jnp.where(upper, came, x), jnp.where(upper, x, came)], axis=axis)

    dones = []
    pieces = []
    late = []
    for j, step in gather_plan(bits):
        order = kinds[uses[j]]
        with jax.named_scope(f"ag{j}{step}"):
            came = held_back(flip(held[j], order[step]), dones[-1:])
            if step > 1 or order[step] != 1:
                held[j] = join(held[j], came, order[step])
                dones.append(held[j])
            else:
                dones.append(came)
            if step == 1 and order[step] == 1:
                for y, x in enumerate((held[j], came)):
                    x = x.reshape(far, block, -1)
                    keep = late if y and j == GATHER[-1] else pieces
                    keep += [(x, y, 0, edges[j]), (flip(x, order[0]), y, 1, edges[j])]
            elif step == 1:
                x = held[j].reshape(2, far, block, -1)
                pieces += [(x, None, 0, edges[j]), (flip(x, order[0]), None, 1, edges[j])]
    out = put(pieces, None, far, block, width)
    out = put(late, out, far, block, width)
    return (out.reshape(parts * block, width), stream)


def solution(mesh):
    in_specs = (
        P("groups", "tp"),
        P("tp", "groups", None),
        P("groups"),
        P("tp", None),
        P(("groups", "tp"), None),
        P("tp", "groups", None),
        P("groups", None),
        P(),
    )
    out_specs = (P("groups", None), P(("groups", "tp"), None))
    return jax.shard_map(
        per_device, mesh=mesh, in_specs=in_specs, out_specs=out_specs, check_vma=False
    )
```

```python
import functools

import jax
import jax.numpy as jnp
from jax import lax
from jax.experimental import pallas as pl
from jax.experimental.pallas import tpu as pltpu
from jax.sharding import PartitionSpec as P

SCATTER = ((4, 1), (5, 0), (4, 0), (3, 0))
GATHER = ((2, 0), (4, 0), (4, 1), (6, 0))
KEY_BLOCK = 2048
TILE = 1024
CODE_TOP = 448.0
LOG2E = 1.4426950408889634


def powers(exps):
    magnitude = jnp.abs(exps)
    result = jnp.ones(exps.shape, jnp.float32)
    for bit in range(6):
        chosen = (magnitude >> bit) & 1 == 1
        result = result * jnp.where(chosen, jnp.float32(2.0**2**bit), jnp.float32(1.0))
    return jnp.where(exps < 0, 1.0 / result, result)


def partial_kernel(
    start_ref, q_ref, kv_ref, exp_ref, weight_ref, *refs, key_block, heads, head, kinds, orders, edges
):
    n_chunks = len(kinds)
    outs = [(refs[2 * j], refs[2 * j + 1]) for j in range(n_chunks)]
    top_ref, acc_ref, limit_ref, attn_ref, held_ref, stage_ref, in_sems, out_sems = refs[2 * n_chunks :]
    step = pl.program_id(0)
    start = start_ref[0]
    rows = q_ref.shape[0]
    n_orders, n_blocks = len(orders), 2 ** len(orders[0])
    me = lax.axis_index("tp")
    block = rows // n_blocks
    coef = head**-0.5 * LOG2E
    n_tiles, _, tile = held_ref.shape
    lanes = limit_ref.shape[2]
    group = weight_ref.shape[1] // lanes
    per = tile // group
    half = rows // 2

    def weight_copy(t):
        return pltpu.make_async_copy(
            weight_ref.at[:, pl.ds(pl.multiple_of(t * tile, tile), tile)], held_ref.at[t], in_sems.at[t]
        )

    @pl.when(step == 0)
    def _():
        for t in range(n_tiles):
            weight_copy(t).start()
        top_ref[...] = jnp.full_like(top_ref, -1e30)
        acc_ref[...] = jnp.zeros_like(acc_ref)
        limit = powers(exp_ref[0]) * CODE_TOP
        for i in range(n_blocks):
            for o in range(n_orders):
                to = pl.ds(pl.multiple_of(place_of(i ^ me, orders[o]) * block, block), block)
                limit_ref[o, to, :] = limit[i * block : (i + 1) * block]

    def attend(masked):
        keys = kv_ref[0, :, :head]
        ones = jnp.ones((key_block, head), jnp.bfloat16)
        values = jnp.concatenate([kv_ref[0, :, head:], ones], axis=1)
        if masked:
            row = lax.broadcasted_iota(jnp.int32, (rows, key_block), 0)
            col = lax.broadcasted_iota(jnp.int32, (rows, key_block), 1)
            seen = col - row <= start - step * key_block
        all_scores = []
        for h in range(heads):
            scores = lax.dot_general(
                q_ref[:, h * head : (h + 1) * head],
                keys,
                (((1,), (1,)), ((), ())),
                preferred_element_type=jnp.float32,
            )
            if masked:
                scores = jnp.where(seen, scores, jnp.float32(-1e30))
            all_scores.append(scores)
        for h, scores in enumerate(all_scores):
            before = top_ref[h]
            top = jnp.maximum(before, jnp.max(scores, axis=1, keepdims=True))
            weights = jnp.exp2((scores - top[:, :1]) * coef).astype(jnp.bfloat16)
            fade = jnp.exp2((before - top) * coef)
            got = jnp.dot(weights, values, preferred_element_type=jnp.float32)
            acc_ref[h] = acc_ref[h] * jnp.concatenate([fade, fade], axis=1) + got
            top_ref[h] = top

    first = step * key_block
    past = first + key_block - 1 > start

    @pl.when(jnp.logical_and(past, first <= start + rows - 1))
    def _():
        attend(True)

    @pl.when(jnp.logical_not(past))
    def _():
        attend(False)

    @pl.when(step == pl.num_programs(0) - 1)
    def _():
        for h in range(heads):
            acc = acc_ref[h]
            out = (acc[:, :head] / acc[:, head:]).astype(jnp.bfloat16)
            for i in range(n_blocks):
                for o in range(n_orders):
                    to = pl.ds(pl.multiple_of(place_of(i ^ me, orders[o]) * block, block), block)
                    attn_ref[o, to, h * head : (h + 1) * head] = out[i * block : (i + 1) * block]

        writes = []
        for j in range(n_chunks):
            tiles = range(edges[j] // tile, edges[j + 1] // tile)
            for t in tiles:
                weight_copy(t).wait()
            limit = limit_ref[kinds[j]]
            rel = attn_ref[kinds[j]]
            for t in tiles:
                got = jnp.dot(rel, held_ref[t], preferred_element_type=jnp.float32)
                for b in range(per):
                    cut = slice(b * group, (b + 1) * group)
                    to = slice(t * tile + b * group, t * tile + (b + 1) * group)
                    bound = jnp.broadcast_to(limit[:, t * per + b : t * per + b + 1], (rows, group))
                    part = jnp.minimum(jnp.maximum(got[:, cut], -bound), bound)
                    stage_ref[:, to] = part.astype(jnp.bfloat16)
            for side in range(2):
                write = pltpu.make_async_copy(
                    stage_ref.at[pl.ds(side * half, half), pl.ds(edges[j], edges[j + 1] - edges[j])],
                    outs[j][side],
                    out_sems.at[j, side],
                )
                write.start()
                writes.append(write)
        for write in writes:
            write.wait()


def partials(start, queries, cache, term_exp, out_weight, kinds, orders, edges):
    rows, span = queries.shape
    context, head = cache.shape[1], cache.shape[2] // 2
    heads = span // head
    n_orders = len(orders)
    blocks = term_exp.shape[2]
    width = out_weight.shape[1]
    n_tiles = width // TILE
    key_block = min(KEY_BLOCK * 256 // rows, context)
    half = rows // 2

    def cache_block(step, start_ref):
        return (0, jnp.minimum(step, (start_ref[0] + rows - 1) // key_block), 0)

    def whole(*shape):
        return pl.BlockSpec(shape, lambda step, start_ref: (0,) * len(shape))

    anywhere = pl.BlockSpec(memory_space=pl.ANY)
    got = pl.pallas_call(
        functools.partial(partial_kernel, key_block=key_block, heads=heads, head=head, kinds=kinds, orders=orders, edges=edges
        ),
        grid_spec=pltpu.PrefetchScalarGridSpec(
            num_scalar_prefetch=1,
            grid=(context // key_block,),
            in_specs=[
                whole(rows, span),
                pl.BlockSpec((1, key_block, 2 * head), cache_block),
                whole(1, rows, blocks),
                anywhere,
            ],
            out_specs=[anywhere] * (2 * len(kinds)),
            scratch_shapes=[
                pltpu.VMEM((heads, rows, head), jnp.float32),
                pltpu.VMEM((heads, rows, 2 * head), jnp.float32),
                pltpu.VMEM((n_orders, rows, blocks), jnp.float32),
                pltpu.VMEM((n_orders, rows, span), jnp.bfloat16),
                pltpu.VMEM((n_tiles, span, TILE), jnp.bfloat16),
                pltpu.VMEM((rows, width), jnp.bfloat16),
                pltpu.SemaphoreType.DMA((n_tiles,)),
                pltpu.SemaphoreType.DMA((len(kinds), 2)),
            ],
        ),
        out_shape=[
            jax.ShapeDtypeStruct((half, edges[i // 2 + 1] - edges[i // 2]), jnp.bfloat16)
            for i in range(2 * len(kinds))
        ],
        compiler_params=pltpu.CompilerParams(vmem_limit_bytes=58 << 20),
        name="partials",
    )(start, queries, cache, term_exp, out_weight)
    return [(got[2 * j], got[2 * j + 1]) for j in range(len(kinds))]


def place_of(index, order):
    top = len(order) - 1
    return sum(((index >> b) & 1) << (top - k) for k, b in enumerate(order))


def put_kernel(*refs, places):
    n = len(places)
    out_ref, stages = refs[-3 - n], refs[-2 - n : -2]
    in_sems, out_sems = refs[-2:]
    me = lax.axis_index("tp")
    reads, writes = [], []
    for i, (at, side, y, core, first) in enumerate(places):
        source = refs[at] if side is None else refs[at].at[side]
        cols = source.shape[-1]
        y = side if y is None else ((me >> 1) & 1) ^ y
        there = out_ref.at[:, y, (me & 1) ^ core, :, pl.ds(first, cols)]
        reads.append(pltpu.make_async_copy(source, stages[i], in_sems.at[i]))
        writes.append(pltpu.make_async_copy(stages[i], there, out_sems.at[i]))
    for read in reads:
        read.start()
    for read, write in zip(reads, writes):
        read.wait()
        write.start()
    for write in writes:
        write.wait()


def put(pieces, out, far, block, width):
    sources, places = [], []
    for array, y, core, first in pieces:
        for side in (None,) if y is not None else range(2):
            places.append((len(sources), side, y, core, first))
        sources.append(array)
    n = len(places)
    sizes = [sources[place[0]].shape[-1] for place in places]
    anywhere = pl.BlockSpec(memory_space=pl.ANY)
    given = sources + ([] if out is None else [out])
    return pl.pallas_call(
        functools.partial(put_kernel, places=places),
        in_specs=[anywhere] * len(given),
        out_specs=anywhere,
        scratch_shapes=[pltpu.VMEM((far, block, cols), sources[0].dtype) for cols in sizes]
        + [
            pltpu.SemaphoreType.DMA((n,)),
            pltpu.SemaphoreType.DMA((n,)),
        ],
        out_shape=jax.ShapeDtypeStruct((far, 2, 2, block, width), sources[0].dtype),
        input_output_aliases={} if out is None else {len(sources): 0},
        compiler_params=pltpu.CompilerParams(vmem_limit_bytes=40 << 20),
        cost_estimate=pl.CostEstimate(
            flops=0, bytes_accessed=4 * far * block * sum(sizes), transcendentals=0
        ),
        name="put",
    )(*given)


def scatter_plan(bits):
    last = bits - 1
    far = list(range(2, last))
    plan = [(0, 0), (1, 0), (2, 0), (3, 0), (0, 1), (1, 1)] + [(0, s) for s in far]
    plan += [(2, 1)] + [(1, s) for s in far] + [(3, 1)]
    plan += [(1, last)] + [(2, s) for s in far] + [(0, last), (2, last)] + [(3, s) for s in far] + [(3, last)]
    return plan


def gather_plan(bits):
    last = bits - 1
    far = list(range(last - 1, 1, -1))
    plan = [(0, last), (2, last)] + [(0, s) for s in far]
    plan += [(1, last)] + [(1, s) for s in far] + [(0, 1), (3, last)] + [(3, s) for s in far]
    plan += [(2, s) for s in far] + [(1, 1), (2, 1), (3, 1)]
    return plan


def edges_of(chunks, width):
    parts = sum(w for w, _ in chunks)
    return [width * sum(w for w, _ in chunks[:j]) // parts for j in range(len(chunks) + 1)]


def per_device(queries, cache, offset, out_weight, residual, term_exp, code_exp, gain):
    me = lax.axis_index("tp")
    parts = lax.axis_size("tp")
    bits = parts.bit_length() - 1
    block, width = residual.shape
    blocks = code_exp.shape[1]
    group = width // blocks
    edges = edges_of(SCATTER, width)

    def flip(x, b):
        return lax.ppermute(x, "tp", [(i, i ^ (1 << b)) for i in range(parts)])

    order_a = list(range(bits))
    order_b = [0] + list(range(2, bits)) + [1]
    kinds = [order_a, order_b]
    uses = [kind for _, kind in SCATTER]

    state = partials(offset, queries, cache, term_exp, out_weight, uses, kinds, edges)

    def held_back(x, others):
        return lax.optimization_barrier((x,) + tuple(others))[0] if others else x

    def merge(keep, came, last=False):
        if last:
            return keep.astype(jnp.float32) + came.astype(jnp.float32), None
        half = keep.shape[0] // 2
        send = (keep[half:].astype(jnp.float32) + came[half:].astype(jnp.float32)).astype(jnp.bfloat16)
        keep = (keep[:half].astype(jnp.float32) + came[:half].astype(jnp.float32)).astype(jnp.bfloat16)
        return keep, send

    last = bits - 1
    dones = []
    for j, step in scatter_plan(bits):
        keep, send = state[j]
        with jax.named_scope(f"rs{j}{step}"):
            came = held_back(flip(send, kinds[uses[j]][step]), dones[-1:])
            state[j] = merge(keep, came, step == last)
            dones.append(state[j][0 if step == last else 1])
    sums = [state[j][0] for j in range(len(SCATTER))]
    summed = jnp.concatenate(sums, axis=1)
    stream = (summed + residual.astype(jnp.float32)).astype(jnp.bfloat16)
    wide = stream.astype(jnp.float32)
    inverse = lax.rsqrt(jnp.mean(wide * wide, axis=1, keepdims=True) + 1e-05)
    exps = lax.dynamic_slice_in_dim(code_exp, me * block, block, 0)
    cap = (powers(exps) * CODE_TOP)[:, :, None]
    normed = (wide * inverse * gain[None, :]).reshape(block, blocks, group)
    mixed = jnp.clip(normed, -cap, cap).reshape(block, width).astype(jnp.bfloat16)

    ones = (1,) * (bits - 1)
    edges = edges_of(GATHER, width)
    held = {j: mixed[:, edges[j] : edges[j + 1]].reshape(ones + (block, -1)) for j in range(len(GATHER))}
    far = parts // 4

    def join(x, came, b):
        upper = (me >> b) & 1 == 1
        axis = 0 if b == 1 else bits - b
        return jnp.concatenate([jnp.where(upper, came, x), jnp.where(upper, x, came)], axis=axis)

    dones = []
    pieces = []
    late = []
    for j, step in gather_plan(bits):
        order = kinds[GATHER[j][1]]
        with jax.named_scope(f"ag{j}{step}"):
            came = held_back(flip(held[j], order[step]), dones[-1:])
            if step > 1 or order[step] != 1:
                held[j] = join(held[j], came, order[step])
                dones.append(held[j])
            else:
                dones.append(came)
            if step == 1 and order[step] == 1:
                for y, x in enumerate((held[j], came)):
                    x = x.reshape(far, block, -1)
                    keep = late if y and j == len(GATHER) - 1 else pieces
                    keep += [(x, y, 0, edges[j]), (flip(x, order[0]), y, 1, edges[j])]
            elif step == 1:
                x = held[j].reshape(2, far, block, -1)
                pieces += [(x, None, 0, edges[j]), (flip(x, order[0]), None, 1, edges[j])]
    out = put(pieces, None, far, block, width)
    out = put(late, out, far, block, width)
    return (out.reshape(parts * block, width), stream)


def solution(mesh):
    in_specs = (
        P("groups", "tp"),
        P("tp", "groups", None),
        P("groups"),
        P("tp", None),
        P(("groups", "tp"), None),
        P("tp", "groups", None),
        P("groups", None),
        P(),
    )
    out_specs = (P("groups", None), P(("groups", "tp"), None))
    return jax.shard_map(
        per_device, mesh=mesh, in_specs=in_specs, out_specs=out_specs, check_vma=False
    )
```

```python
import functools

import jax
import jax.numpy as jnp
from jax import lax
from jax.experimental import pallas as pl
from jax.experimental.pallas import tpu as pltpu
from jax.sharding import PartitionSpec as P

SCATTER = ((4, 1), (5, 0), (4, 0), (3, 0))
GATHER = ((2, 0), (4, 0), (4, 1), (6, 0))
KEY_BLOCK = 2048
TILE = 1024
CODE_TOP = 448.0
LOG2E = 1.4426950408889634


def powers(exps):
    magnitude = jnp.abs(exps)
    result = jnp.ones(exps.shape, jnp.float32)
    for bit in range(6):
        chosen = (magnitude >> bit) & 1 == 1
        result = result * jnp.where(chosen, jnp.float32(2.0**2**bit), jnp.float32(1.0))
    return jnp.where(exps < 0, 1.0 / result, result)


def partial_kernel(
    start_ref, q_ref, kv_ref, exp_ref, weight_ref, *refs, key_block, heads, head, kinds, orders, edges
):
    n_chunks = len(kinds)
    outs = [(refs[2 * j], refs[2 * j + 1]) for j in range(n_chunks)]
    top_ref, acc_ref, limit_ref, attn_ref, held_ref, stage_ref, in_sems, out_sems = refs[2 * n_chunks :]
    step = pl.program_id(0)
    start = start_ref[0]
    rows = q_ref.shape[0]
    n_orders, n_blocks = len(orders), 2 ** len(orders[0])
    me = lax.axis_index("tp")
    block = rows // n_blocks
    coef = head**-0.5 * LOG2E
    n_tiles, _, tile = held_ref.shape
    lanes = limit_ref.shape[2]
    group = weight_ref.shape[1] // lanes
    per = tile // group
    half = rows // 2

    def weight_copy(t):
        return pltpu.make_async_copy(
            weight_ref.at[:, pl.ds(pl.multiple_of(t * tile, tile), tile)], held_ref.at[t], in_sems.at[t]
        )

    @pl.when(step == 0)
    def _():
        for t in range(n_tiles):
            weight_copy(t).start()
        top_ref[...] = jnp.full_like(top_ref, -1e30)
        acc_ref[...] = jnp.zeros_like(acc_ref)
        limit = powers(exp_ref[0]) * CODE_TOP
        for i in range(n_blocks):
            for o in range(n_orders):
                to = pl.ds(pl.multiple_of(place_of(i ^ me, orders[o]) * block, block), block)
                limit_ref[o, to, :] = limit[i * block : (i + 1) * block]

    def attend(masked):
        keys = kv_ref[0, :, :head]
        ones = jnp.ones((key_block, head), jnp.bfloat16)
        values = jnp.concatenate([kv_ref[0, :, head:], ones], axis=1)
        if masked:
            row = lax.broadcasted_iota(jnp.int32, (rows, key_block), 0)
            col = lax.broadcasted_iota(jnp.int32, (rows, key_block), 1)
            seen = col - row <= start - step * key_block
        all_scores = []
        for h in range(heads):
            scores = lax.dot_general(
                q_ref[:, h * head : (h + 1) * head],
                keys,
                (((1,), (1,)), ((), ())),
                preferred_element_type=jnp.float32,
            )
            if masked:
                scores = jnp.where(seen, scores, jnp.float32(-1e30))
            all_scores.append(scores)
        for h, scores in enumerate(all_scores):
            before = top_ref[h]
            top = jnp.maximum(before, jnp.max(scores, axis=1, keepdims=True))
            weights = jnp.exp2((scores - top[:, :1]) * coef).astype(jnp.bfloat16)
            fade = jnp.exp2((before - top) * coef)
            got = jnp.dot(weights, values, preferred_element_type=jnp.float32)
            acc_ref[h] = acc_ref[h] * jnp.concatenate([fade, fade], axis=1) + got
            top_ref[h] = top

    first = step * key_block
    past = first + key_block - 1 > start

    @pl.when(jnp.logical_and(past, first <= start + rows - 1))
    def _():
        attend(True)

    @pl.when(jnp.logical_not(past))
    def _():
        attend(False)

    @pl.when(step == pl.num_programs(0) - 1)
    def _():
        for h in range(heads):
            acc = acc_ref[h]
            out = (acc[:, :head] / acc[:, head:]).astype(jnp.bfloat16)
            for i in range(n_blocks):
                for o in range(n_orders):
                    to = pl.ds(pl.multiple_of(place_of(i ^ me, orders[o]) * block, block), block)
                    attn_ref[o, to, h * head : (h + 1) * head] = out[i * block : (i + 1) * block]

        writes = []
        for j in range(n_chunks):
            tiles = range(edges[j] // tile, edges[j + 1] // tile)
            for t in tiles:
                weight_copy(t).wait()
            limit = limit_ref[kinds[j]]
            rel = attn_ref[kinds[j]]
            for t in tiles:
                got = jnp.dot(rel, held_ref[t], preferred_element_type=jnp.float32)
                for b in range(per):
                    cut = slice(b * group, (b + 1) * group)
                    to = slice(t * tile + b * group, t * tile + (b + 1) * group)
                    bound = jnp.broadcast_to(limit[:, t * per + b : t * per + b + 1], (rows, group))
                    part = jnp.minimum(jnp.maximum(got[:, cut], -bound), bound)
                    stage_ref[:, to] = part.astype(jnp.bfloat16)
            for side in range(2):
                write = pltpu.make_async_copy(
                    stage_ref.at[pl.ds(side * half, half), pl.ds(edges[j], edges[j + 1] - edges[j])],
                    outs[j][side],
                    out_sems.at[j, side],
                )
                write.start()
                writes.append(write)
        for write in writes:
            write.wait()


def partials(start, queries, cache, term_exp, out_weight, kinds, orders, edges):
    rows, span = queries.shape
    context, head = cache.shape[1], cache.shape[2] // 2
    heads = span // head
    n_orders = len(orders)
    blocks = term_exp.shape[2]
    width = out_weight.shape[1]
    n_tiles = width // TILE
    key_block = min(KEY_BLOCK * 256 // rows, context)
    half = rows // 2

    def cache_block(step, start_ref):
        return (0, jnp.minimum(step, (start_ref[0] + rows - 1) // key_block), 0)

    def whole(*shape):
        return pl.BlockSpec(shape, lambda step, start_ref: (0,) * len(shape))

    anywhere = pl.BlockSpec(memory_space=pl.ANY)
    got = pl.pallas_call(
        functools.partial(partial_kernel, key_block=key_block, heads=heads, head=head, kinds=kinds, orders=orders, edges=edges
        ),
        grid_spec=pltpu.PrefetchScalarGridSpec(
            num_scalar_prefetch=1,
            grid=(context // key_block,),
            in_specs=[
                whole(rows, span),
                pl.BlockSpec((1, key_block, 2 * head), cache_block),
                whole(1, rows, blocks),
                anywhere,
            ],
            out_specs=[anywhere] * (2 * len(kinds)),
            scratch_shapes=[
                pltpu.VMEM((heads, rows, head), jnp.float32),
                pltpu.VMEM((heads, rows, 2 * head), jnp.float32),
                pltpu.VMEM((n_orders, rows, blocks), jnp.float32),
                pltpu.VMEM((n_orders, rows, span), jnp.bfloat16),
                pltpu.VMEM((n_tiles, span, TILE), jnp.bfloat16),
                pltpu.VMEM((rows, width), jnp.bfloat16),
                pltpu.SemaphoreType.DMA((n_tiles,)),
                pltpu.SemaphoreType.DMA((len(kinds), 2)),
            ],
        ),
        out_shape=[
            jax.ShapeDtypeStruct((half, edges[i // 2 + 1] - edges[i // 2]), jnp.bfloat16)
            for i in range(2 * len(kinds))
        ],
        compiler_params=pltpu.CompilerParams(vmem_limit_bytes=58 << 20),
        name="partials",
    )(start, queries, cache, term_exp, out_weight)
    return [(got[2 * j], got[2 * j + 1]) for j in range(len(kinds))]


def place_of(index, order):
    top = len(order) - 1
    return sum(((index >> b) & 1) << (top - k) for k, b in enumerate(order))


def put_kernel(*refs, places):
    n = len(places)
    out_ref, stages = refs[-3 - n], refs[-2 - n : -2]
    in_sems, out_sems = refs[-2:]
    me = lax.axis_index("tp")
    reads, writes = [], []
    for i, (at, side, y, core, first) in enumerate(places):
        source = refs[at] if side is None else refs[at].at[side]
        cols = source.shape[-1]
        y = side if y is None else ((me >> 1) & 1) ^ y
        there = out_ref.at[:, y, (me & 1) ^ core, :, pl.ds(first, cols)]
        reads.append(pltpu.make_async_copy(source, stages[i], in_sems.at[i]))
        writes.append(pltpu.make_async_copy(stages[i], there, out_sems.at[i]))
    for read in reads:
        read.start()
    for read, write in zip(reads, writes):
        read.wait()
        write.start()
    for write in writes:
        write.wait()


def put(pieces, out, far, block, width):
    sources, places = [], []
    for array, y, core, first in pieces:
        for side in (None,) if y is not None else range(2):
            places.append((len(sources), side, y, core, first))
        sources.append(array)
    n = len(places)
    sizes = [sources[place[0]].shape[-1] for place in places]
    anywhere = pl.BlockSpec(memory_space=pl.ANY)
    given = sources + ([] if out is None else [out])
    return pl.pallas_call(
        functools.partial(put_kernel, places=places),
        in_specs=[anywhere] * len(given),
        out_specs=anywhere,
        scratch_shapes=[pltpu.VMEM((far, block, cols), sources[0].dtype) for cols in sizes]
        + [
            pltpu.SemaphoreType.DMA((n,)),
            pltpu.SemaphoreType.DMA((n,)),
        ],
        out_shape=jax.ShapeDtypeStruct((far, 2, 2, block, width), sources[0].dtype),
        input_output_aliases={} if out is None else {len(sources): 0},
        compiler_params=pltpu.CompilerParams(vmem_limit_bytes=40 << 20),
        cost_estimate=pl.CostEstimate(
            flops=0, bytes_accessed=4 * far * block * sum(sizes), transcendentals=0
        ),
        name="put",
    )(*given)


def scatter_plan(bits):
    last = bits - 1
    far = list(range(2, last))
    plan = [(0, 0), (1, 0), (2, 0), (3, 0), (0, 1), (1, 1)] + [(0, s) for s in far]
    plan += [(2, 1)] + [(1, s) for s in far] + [(3, 1)]
    plan += [(1, last)] + [(2, s) for s in far] + [(0, last), (2, last)] + [(3, s) for s in far] + [(3, last)]
    return plan


def gather_plan(bits):
    last = bits - 1
    far = list(range(last - 1, 1, -1))
    plan = [(0, last), (2, last)] + [(0, s) for s in far]
    plan += [(1, last)] + [(1, s) for s in far] + [(0, 1), (3, last)] + [(3, s) for s in far]
    plan += [(2, s) for s in far] + [(1, 1), (2, 1), (3, 1)]
    return plan


def edges_of(chunks, width):
    parts = sum(w for w, _ in chunks)
    return [width * sum(w for w, _ in chunks[:j]) // parts for j in range(len(chunks) + 1)]


def per_device(queries, cache, offset, out_weight, residual, term_exp, code_exp, gain):
    me = lax.axis_index("tp")
    parts = lax.axis_size("tp")
    bits = parts.bit_length() - 1
    block, width = residual.shape
    blocks = code_exp.shape[1]
    group = width // blocks
    edges = edges_of(SCATTER, width)

    def flip(x, b):
        return lax.ppermute(x, "tp", [(i, i ^ (1 << b)) for i in range(parts)])

    order_a = list(range(bits))
    order_b = [0] + list(range(2, bits)) + [1]
    kinds = [order_a, order_b]
    uses = [kind for _, kind in SCATTER]

    state = partials(offset, queries, cache, term_exp, out_weight, uses, kinds, edges)

    def held_back(x, others):
        return lax.optimization_barrier((x,) + tuple(others))[0] if others else x

    def merge(keep, came, last=False):
        if last:
            return keep.astype(jnp.float32) + came.astype(jnp.float32), None
        half = keep.shape[0] // 2
        send = (keep[half:].astype(jnp.float32) + came[half:].astype(jnp.float32)).astype(jnp.bfloat16)
        keep = (keep[:half].astype(jnp.float32) + came[:half].astype(jnp.float32)).astype(jnp.bfloat16)
        return keep, send

    last = bits - 1
    dones = []
    for j, step in scatter_plan(bits):
        keep, send = state[j]
        with jax.named_scope(f"rs{j}{step}"):
            came = held_back(flip(send, kinds[uses[j]][step]), dones[-1:])
            state[j] = merge(keep, came, step == last)
            dones.append(state[j][0 if step == last else 1])
    sums = [state[j][0] for j in range(len(SCATTER))]
    summed = jnp.concatenate(sums, axis=1)
    stream = (summed + residual.astype(jnp.float32)).astype(jnp.bfloat16)
    wide = stream.astype(jnp.float32)
    inverse = lax.rsqrt(jnp.mean(wide * wide, axis=1, keepdims=True) + 1e-05)
    exps = lax.dynamic_slice_in_dim(code_exp, me * block, block, 0)
    cap = jnp.broadcast_to((powers(exps) * CODE_TOP)[:, :, None], (block, blocks, group))
    cap = lax.optimization_barrier(cap)
    normed = (wide * inverse * gain[None, :]).reshape(block, blocks, group)
    mixed = jnp.clip(normed, -cap, cap).reshape(block, width).astype(jnp.bfloat16)

    ones = (1,) * (bits - 1)
    edges = edges_of(GATHER, width)
    held = {j: mixed[:, edges[j] : edges[j + 1]].reshape(ones + (block, -1)) for j in range(len(GATHER))}
    far = parts // 4

    def join(x, came, b):
        upper = (me >> b) & 1 == 1
        axis = 0 if b == 1 else bits - b
        return jnp.concatenate([jnp.where(upper, came, x), jnp.where(upper, x, came)], axis=axis)

    dones = []
    pieces = []
    late = []
    for j, step in gather_plan(bits):
        order = kinds[GATHER[j][1]]
        with jax.named_scope(f"ag{j}{step}"):
            came = held_back(flip(held[j], order[step]), dones[-1:])
            if step > 1 or order[step] != 1:
                held[j] = join(held[j], came, order[step])
                dones.append(held[j])
            else:
                dones.append(came)
            if step == 1 and order[step] == 1:
                for y, x in enumerate((held[j], came)):
                    x = x.reshape(far, block, -1)
                    keep = late if y and j == len(GATHER) - 1 else pieces
                    keep += [(x, y, 0, edges[j]), (flip(x, order[0]), y, 1, edges[j])]
            elif step == 1:
                x = held[j].reshape(2, far, block, -1)
                pieces += [(x, None, 0, edges[j]), (flip(x, order[0]), None, 1, edges[j])]
    out = put(pieces, None, far, block, width)
    out = put(late, out, far, block, width)
    return (out.reshape(parts * block, width), stream)


def solution(mesh):
    in_specs = (
        P("groups", "tp"),
        P("tp", "groups", None),
        P("groups"),
        P("tp", None),
        P(("groups", "tp"), None),
        P("tp", "groups", None),
        P("groups", None),
        P(),
    )
    out_specs = (P("groups", None), P(("groups", "tp"), None))
    return jax.shard_map(
        per_device, mesh=mesh, in_specs=in_specs, out_specs=out_specs, check_vma=False
    )
```
